32 devices in a mesh: row: 16 (over z, y, x), col: 2 (over core).
Axes of the slice: x: 2, y: 2, z: 4, core: 2. Of those that a mesh axis runs over, the one named last changes fastest.
Arguments:
- eigenvectors: float32 [2, 20480, 1024], P(None, 'row', 'col'), may hold values from -6 to 6
- reflectors: float32 [4, 2, 20480, 128], P(None, None, 'row', 'col'), may hold values from -0.03125 to 0.03125
- reflector_factors: float32 [4, 2, 128, 128], replicated, as said below
Outputs:
- transformed: float32 [2, 20480, 1024], P(None, 'row', 'col')
The draws below stay inside these ranges and needn't reach their ends.
Inputs may be any that keep to these rules, and one draw needn't show every extreme that they name: Each block of reflector_factors is upper triangular in both parts; the real part of its diagonal lies between 1 and 2.
All inputs are finite; a program needn't handle non-finite values.
Results may differ from the reference program's by a relative error of at most 0.00017.
Values sent between devices are 32-bit elements; how exact they have to be, the bound alone decides.
A program may use at most 128 MiB of HBM per device.

```python
import jax
import jax.numpy as jnp
from jax import lax

N = 20480
W = 128
NB = 4
M = 1024


def draw_reflector_factors(key, part):
    key = jax.random.fold_in(key, 11)
    key_off, key_real, key_imag = jax.random.split(key, 3)
    low_end, spread = (1.0, 0.5)
    row_ids = jnp.arange(W)[:, None]
    col_ids = jnp.arange(W)[None, :]
    upper = (col_ids > row_ids).astype(jnp.float32)
    identity = (col_ids == row_ids).astype(jnp.float32)
    off_part = jax.random.uniform(key_off, (NB, 2, W, W), jnp.float32, -1.0, 1.0) * (spread * 1.7320508 / W ** 0.5)
    diag_real = jax.random.uniform(key_real, (NB, W), jnp.float32, low_end, 2.0)
    diag_imag = jax.random.uniform(key_imag, (NB, W), jnp.float32, -0.5, 0.5)
    diag_both = jnp.stack([diag_real, diag_imag], axis=1)
    return off_part * upper + identity * diag_both[:, :, None, :]


def steps_of(rng, shape, shards, least, top_value):
    def one(position, parts):
        heights = jax.random.uniform(jax.random.fold_in(jax.random.fold_in(rng, 6), position), (parts,), jnp.float32, least / len(shards), top_value / len(shards))
        return jnp.repeat(jnp.exp(heights), shape[position] // parts).reshape((-1,) + (1,) * (len(shape) - position - 1))

    loudness = one(*shards[0])
    for cut in shards[1:]:
        loudness = loudness * one(*cut)
    return loudness


def bell_draw(stream_key, shape, width, limit, pieces=(), kind=jnp.bfloat16):
    result = width * jax.random.normal(stream_key, shape, jnp.float32)
    if pieces:
        result = result * steps_of(stream_key, shape, pieces, -0.22, 0.18)
    return jnp.clip(result, -limit, limit).astype(kind)


def setup_inputs(seed: int = 0) -> dict:
    keys = jax.random.split(jax.random.key(seed), 4)
    return {
        "eigenvectors": bell_draw(keys[0], (2, N, M), 1.0, 6.0, ((1, 16), (2, 2)), jnp.float32),
        "reflectors": bell_draw(keys[1], (NB, 2, N, W), (2 * N) ** -0.5, 0.03125, ((2, 16), (3, 2)), jnp.float32),
        "reflector_factors": draw_reflector_factors(jax.random.fold_in(keys[3], 71), 0),
    }


def complex_product(left_side, right_side):
    real_part = jnp.dot(left_side[0], right_side[0], precision=lax.Precision.HIGHEST) - jnp.dot(left_side[1], right_side[1], precision=lax.Precision.HIGHEST)
    imag_part = jnp.dot(left_side[0], right_side[1], precision=lax.Precision.HIGHEST) + jnp.dot(left_side[1], right_side[0], precision=lax.Precision.HIGHEST)
    return jnp.stack([real_part, imag_part])


def adjoint_product(left_side, right_side):
    real_part = jnp.dot(left_side[0].T, right_side[0], precision=lax.Precision.HIGHEST) + jnp.dot(left_side[1].T, right_side[1], precision=lax.Precision.HIGHEST)
    imag_part = jnp.dot(left_side[0].T, right_side[1], precision=lax.Precision.HIGHEST) - jnp.dot(left_side[1].T, right_side[0], precision=lax.Precision.HIGHEST)
    return jnp.stack([real_part, imag_part])


def reference(eigenvectors, reflectors, reflector_factors):
    current = eigenvectors
    for block_index in reversed(range(NB)):
        vectors = reflectors[block_index]
        projected = adjoint_product(vectors, current)
        coefficients = complex_product(reflector_factors[block_index], projected)
        current = current - complex_product(vectors, coefficients)
    return current
```

```python
import jax
import jax.numpy as jnp
from jax import lax
from jax.sharding import PartitionSpec as P


def product(spec, left_side, right_side):
    return jnp.einsum(spec, left_side, right_side, precision=lax.Precision.HIGH)


def adjoint_transposed(columns, vectors):
    spec = "nm,...nk->...mk"
    real_part = product(spec, columns[0], vectors[..., 0, :, :]) + product(spec, columns[1], vectors[..., 1, :, :])
    imag_part = product(spec, columns[1], vectors[..., 0, :, :]) - product(spec, columns[0], vectors[..., 1, :, :])
    return jnp.stack([real_part, imag_part], axis=-3)


def complex_rows(spec, left_side, right_side):
    real_part = product(spec, left_side[0], right_side[0]) - product(spec, left_side[1], right_side[1])
    imag_part = product(spec, left_side[0], right_side[1]) + product(spec, left_side[1], right_side[0])
    return jnp.stack([real_part, imag_part])


def merged_shards(eigenvectors, reflectors, reflector_factors):
    block_count, _, rows, share = reflectors.shape
    vectors = lax.all_gather(reflectors, "col", axis=3, tiled=True)
    width = vectors.shape[3]
    grams = []
    for block in range(block_count - 1):
        later = jnp.concatenate([reflectors[c] for c in range(block + 1, block_count)], axis=2)
        grams.append(adjoint_transposed(later, vectors[block]))
    gram = lax.psum(jnp.concatenate(grams, axis=1), "row")
    gram = gram.reshape(2, -1, share, width)
    gram = lax.all_gather(gram, "col", axis=2, tiled=True)
    projected = lax.psum_scatter(
        adjoint_transposed(eigenvectors, vectors), "row", scatter_dimension=2, tiled=True
    )
    results = [None] * block_count
    for block in reversed(range(block_count)):
        start = sum(block_count - 1 - b for b in range(block))
        sums = projected[block]
        for c in range(block + 1, block_count):
            sums = sums - complex_rows("mk,kj->mj", results[c], gram[:, start + c - block - 1])
        results[block] = complex_rows("mk,jk->mj", sums, reflector_factors[block])
    result = lax.all_gather(jnp.concatenate(results, axis=2), "row", axis=1, tiled=True)
    flat = vectors.transpose(1, 2, 0, 3).reshape(2, rows, block_count * width)
    return eigenvectors - complex_rows("nk,mk->nm", flat, result)


def solution(mesh):
    placed = (P(None, "row", "col"), P(None, None, "row", "col"), P())
    return jax.shard_map(
        merged_shards, mesh=mesh, in_specs=placed, out_specs=P(None, "row", "col"), check_vma=False
    )
```

```python
import jax
import jax.numpy as jnp
from jax import lax
from jax.experimental import pallas as pl
from jax.experimental.pallas import tpu as pltpu
from jax.sharding import PartitionSpec as P

F32 = jnp.float32
BF16 = jnp.bfloat16
BITS = 4
GRAM = 4
ORDERS = {3: (0, 1, 2, 3), 2: (1, 2, 0, 3), GRAM: (1, 0, 2, 3), 1: (2, 0, 1, 3), 0: (0, 1, 2, 3)}


def split(value):
    high = value.astype(BF16)
    return high, (value - high.astype(F32)).astype(BF16)


def dot(left, right):
    return jnp.dot(left, right, preferred_element_type=F32)


def dot_lanes(left, right):
    return lax.dot_general(left, right, (((1,), (1,)), ((), ())), preferred_element_type=F32)


def kernel(z_hbm, v_hbm, factors, out_hbm, z, zt, w_own, w_other, vt, forms, acc, gacc,
           slots, gslots, xt, gx, gother, xk, gram, z_sem, v_sem, out_sem, pair_send, pair_recv,
           row_send, row_recv):
    rows, columns = z.shape[1], z.shape[2]
    blocks = w_own.shape[0]
    share = w_own.shape[2] // 2
    row, col = lax.axis_index("row"), lax.axis_index("col")
    mine = [lax.rem(row // (1 << bit), 2) for bit in range(BITS)]
    partner = [row + (1 << bit) * (1 - 2 * mine[bit]) for bit in range(BITS)]
    sibling = {"row": row, "col": 1 - col}

    z_in = [pltpu.make_async_copy(z_hbm.at[p], z.at[p], z_sem.at[p]) for p in range(2)]
    v_in = [pltpu.make_async_copy(v_hbm.at[b], w_own.at[b], v_sem.at[b]) for b in range(blocks)]
    for b in reversed(range(blocks)):
        v_in[b].start()
    for copy in z_in:
        copy.start()

    barrier = pltpu.get_barrier_semaphore()
    for bit in range(BITS):
        pl.semaphore_signal(barrier, inc=1, device_id={"row": partner[bit], "col": col},
                            device_id_type=pl.DeviceIdType.MESH)
    pl.semaphore_signal(barrier, inc=1, device_id=sibling, device_id_type=pl.DeviceIdType.MESH)
    pl.semaphore_wait(barrier, BITS + 1)

    sends = []

    def send(source, target, send_sem, recv_sem, device):
        copy = pltpu.make_async_remote_copy(
            src_ref=source, dst_ref=target, send_sem=send_sem, recv_sem=recv_sem,
            device_id=device, device_id_type=pl.DeviceIdType.MESH)
        copy.start()
        sends.append(copy)
        return copy

    v_copies = {}
    for b in reversed(range(blocks)):
        v_in[b].wait()
        v_copies[b] = send(w_own.at[b], w_other.at[b], pair_send.at[b], pair_recv.at[b], sibling)

    @pl.loop(0, rows // 128)
    def _(step):
        part = pl.ds(pl.multiple_of(step * 128, 128), 128)
        for b in range(blocks):
            high, low = split(w_own[b, part, :].T)
            for p in range(2):
                vt[0, p, b * share:(b + 1) * share, part] = high[p * share:(p + 1) * share]
                vt[1, p, b * share:(b + 1) * share, part] = low[p * share:(p + 1) * share]

    for copy in z_in:
        copy.wait()

    @pl.loop(0, rows // 128)
    def _(step):
        part = pl.ds(pl.multiple_of(step * 128, 128), 128)
        for p in range(2):
            high, low = split(z[p, part, :].T)
            zt[0, p, :, part] = high
            zt[1, p, :, part] = low

    lane = lax.broadcasted_iota(jnp.int32, (1, 128), 1)
    sign = jnp.where(lane < share, 1.0, -1.0).astype(F32)

    def make_forms(b):
        v_copies[b].wait_recv()

        @pl.loop(0, rows // 256)
        def _(step):
            part = pl.ds(pl.multiple_of(step * 256, 256), 256)
            own, other = w_own[b, part, :], w_other[b, part, :]
            halves = (jnp.where(col == 0, own, other), jnp.where(col == 0, other, own))
            for h in range(2):
                lanes = slice(b * 256 + h * 128, b * 256 + h * 128 + 128)
                for form, value in ((0, halves[h] * sign), (1, pltpu.roll(halves[h], share, 1))):
                    high, low = split(value)
                    forms[form, 0, part, lanes] = high
                    forms[form, 1, part, lanes] = low

    def products(turned, b, first, count):
        def body(step, total):
            part = pl.ds(pl.multiple_of(step * 256, 256), 256)
            for p in range(2):
                high = turned[0, p, first:first + count, part]
                low = turned[1, p, first:first + count, part]
                f_high = forms[p, 0, part, b * 256:(b + 1) * 256]
                f_low = forms[p, 1, part, b * 256:(b + 1) * 256]
                total = total + dot(high, f_high) + dot(high, f_low) + dot(low, f_high)
            return total

        return lax.fori_loop(0, rows // 256, body, jnp.zeros((count, 256), F32))

    def place(ref, prefix, free, fixed):
        at = list(prefix)
        for bit in reversed(range(BITS)):
            at.append(slice(None) if bit in free else fixed[bit])
        return ref.at[tuple(at)]

    def buffers(chunk):
        if chunk == GRAM:
            return gacc, (), gslots, (), gx
        return acc, (chunk,), slots, (chunk,), xt

    pending = {}

    def start_reduce(chunk, step):
        source, prefix, slot, slot_prefix, _ = buffers(chunk)
        order = ORDERS[chunk]
        fixed = dict(enumerate(mine))
        fixed[order[step]] = 1 - mine[order[step]]
        target = slot[step].at[slot_prefix] if slot_prefix else slot[step]
        pending[chunk] = send(
            place(source, prefix, order[step + 1:], fixed), target,
            row_send.at[chunk, step], row_recv.at[chunk, step],
            {"row": partner[order[step]], "col": col})

    def finish_reduce(chunk, step):
        source, prefix, slot, slot_prefix, _ = buffers(chunk)
        order = ORDERS[chunk]
        pending[chunk].wait_recv()
        held = place(source, prefix, order[step + 1:], dict(enumerate(mine)))
        arrived = slot[step].at[slot_prefix] if slot_prefix else slot[step]
        held[...] = held[...] + arrived[...]

    def start_spread(chunk, step):
        _, prefix, _, _, target = buffers(chunk)
        order = ORDERS[chunk][::-1]
        part = place(target, prefix, order[:step], dict(enumerate(mine)))
        pending[chunk] = send(
            part, part, row_send.at[chunk, BITS + step], row_recv.at[chunk, BITS + step],
            {"row": partner[order[step]], "col": col})

    def own_part(ref, prefix):
        return place(ref, prefix, (), dict(enumerate(mine)))

    def finish_gram():
        gram_copy.wait_recv()
        start = 0
        for b in range(blocks - 1):
            for c in range(b + 1, blocks):
                for group in range(share // 8):
                    q = (start * share) // 8 + group
                    owner, sub = q // 3, q % 3
                    at = (owner // 8, (owner // 4) % 2, (owner // 2) % 2, owner % 2, sub)
                    own, other = gx[at], gother[at]
                    halves = (jnp.where(col == 0, own, other), jnp.where(col == 0, other, own))
                    for h in range(2):
                        base = h * 2 * share + group * 8
                        gram[start, base:base + 8, :] = halves[h]
                        turned = jnp.concatenate(
                            [pltpu.roll(halves[h][:, k:k + 128], share, 1) * -sign for k in (0, 128)], axis=1)
                        gram[start, base + share:base + share + 8, :] = turned
                start += 1

    def dot3(left, high, low):
        l_high, l_low = split(left)
        return dot(l_high, high) + dot(l_high, low) + dot(l_low, high)

    solved = {}

    def solve(b):
        sums = own_part(acc, (b,))[...]
        start = sum(blocks - 1 - k for k in range(b))
        for c in range(b + 1, blocks):
            high, low = split(gram[start + c - b - 1])
            sums = sums - dot3(solved[c], high, low)
        high, low = split(factors[b])
        solved[b] = dot3(sums, high, low)
        own_part(xt, (b,))[...] = solved[b]

    stage = {}

    def advance(chunk):
        nonlocal gram_copy
        step = stage[chunk]
        if step < BITS:
            finish_reduce(chunk, step)
            if step + 1 < BITS:
                start_reduce(chunk, step + 1)
            elif chunk == GRAM:
                own_part(gx, ())[...] = own_part(gacc, ())[...]
                start_spread(chunk, 0)
            elif chunk == blocks - 1:
                solve(chunk)
                start_spread(chunk, 0)
        elif step < 2 * BITS:
            pending[chunk].wait_recv()
            if step + 1 < 2 * BITS:
                start_spread(chunk, step + 1 - BITS)
            elif chunk == GRAM:
                gram_copy = send(gx, gother, pair_send.at[GRAM], pair_recv.at[GRAM], sibling)
        stage[chunk] += 1

    gram_copy = None

    def begin(chunk):
        if chunk == GRAM:
            q = 0
            for b in range(blocks - 1):
                count = share * (blocks - 1 - b)
                value = products(vt, b, share * (b + 1), count)
                for group in range(count // 8):
                    owner, sub = q // 3, q % 3
                    gacc[owner // 8, (owner // 4) % 2, (owner // 2) % 2, owner % 2, sub] = (
                        value[group * 8:group * 8 + 8])
                    q += 1
        else:
            value = products(zt, chunk, 0, columns)
            acc[chunk] = value.reshape(acc.shape[1:])
        start_reduce(chunk, 0)
        stage[chunk] = 0

    make_forms(3)
    begin(3)
    make_forms(2)
    begin(2)
    make_forms(1)
    make_forms(0)
    begin(GRAM)
    begin(1)
    advance(3)
    begin(0)
    for chunk in (2, GRAM, 3, 1, 0):
        advance(chunk)
    while stage[GRAM] < 2 * BITS:
        for chunk in (3, 2, GRAM, 1, 0):
            limit = 2 * BITS if chunk in (3, GRAM) else BITS
            if stage[chunk] < limit:
                advance(chunk)
    finish_gram()
    for b in (2, 1, 0):
        solve(b)
        start_spread(b, 0)

    def take(b):
        high, low = split(xt[b].reshape(columns, 256))
        xk[0, :, b * 256:(b + 1) * 256] = high
        xk[1, :, b * 256:(b + 1) * 256] = low

    def update(first, count, last):
        lanes = slice(first * 256, (first + count) * 256)

        @pl.loop(0, rows // 256)
        def _(step):
            part = pl.ds(pl.multiple_of(step * 256, 256), 256)
            for p in range(2):
                f_high, f_low = forms[p, 0, part, lanes], forms[p, 1, part, lanes]
                x_high, x_low = xk[0, :, lanes], xk[1, :, lanes]
                z[p, part, :] = z[p, part, :] - (
                    dot_lanes(f_high, x_high) + dot_lanes(f_high, x_low) + dot_lanes(f_low, x_high))
                if last:
                    pltpu.make_async_copy(
                        z.at[p, part, :], out_hbm.at[p, part, :], out_sem.at[p, step]).start()

    for _ in range(BITS - 1):
        for b in (2, 1, 0):
            advance(b)
    advance(2)
    take(3)
    take(2)
    update(2, 2, False)
    advance(1)
    advance(0)
    take(1)
    take(0)
    update(0, 2, True)
    for copy in sends:
        copy.wait_send()

    @pl.loop(0, rows // 256)
    def _(step):
        part = pl.ds(pl.multiple_of(step * 256, 256), 256)
        for p in range(2):
            pltpu.make_async_copy(z.at[p, part, :], out_hbm.at[p, part, :], out_sem.at[p, step]).wait()


def fused_shards(eigenvectors, reflectors, reflector_factors):
    blocks, _, rows, share = reflectors.shape
    columns = eigenvectors.shape[2]
    width = reflector_factors.shape[2]
    packed = jnp.concatenate([reflectors[:, 0], reflectors[:, 1]], axis=2)
    turned = jnp.swapaxes(reflector_factors, 2, 3)
    whole = jnp.stack([turned, jnp.stack([-turned[:, 1], turned[:, 0]], axis=1)], axis=1)
    whole = whole.reshape(blocks, 2, 2, 2, share, 2, share).transpose(0, 3, 1, 4, 5, 2, 6)
    whole = whole.reshape(blocks, 2 * width, 2 * width)
    two = (2,) * BITS
    owned = columns // 2 ** BITS
    vmem = pltpu.VMEM
    dma = pltpu.SemaphoreType.DMA
    slot_shapes = [vmem((blocks,) + (2,) * (BITS - 1 - s) + (owned, 2 * width), F32) for s in range(BITS)]
    gslot_shapes = [vmem((2,) * (BITS - 1 - s) + (3, 8, 2 * width), F32) for s in range(BITS)]
    scratch = [
        vmem((2, rows, columns), F32),
        vmem((2, 2, columns, rows), BF16),
        vmem((blocks, rows, width), F32),
        vmem((blocks, rows, width), F32),
        vmem((2, 2, blocks * share, rows), BF16),
        vmem((2, 2, rows, blocks * 2 * width), BF16),
        vmem((blocks,) + two + (owned, 2 * width), F32),
        vmem(two + (3, 8, 2 * width), F32),
        slot_shapes,
        gslot_shapes,
        vmem((blocks,) + two + (owned, 2 * width), F32),
        vmem(two + (3, 8, 2 * width), F32),
        vmem(two + (3, 8, 2 * width), F32),
        vmem((2, columns, blocks * 2 * width), BF16),
        vmem((6, 2 * width, 2 * width), F32),
        dma((2,)),
        dma((blocks,)),
        dma((2, rows // 256)),
        dma((blocks + 1,)),
        dma((blocks + 1,)),
        dma((blocks + 1, 2 * BITS)),
        dma((blocks + 1, 2 * BITS)),
    ]
    anywhere = pl.BlockSpec(memory_space=pl.ANY)
    near = pl.BlockSpec(memory_space=pltpu.VMEM)
    flops = 2 * 2 * 3 * 4 * blocks * width * rows * columns
    return pl.pallas_call(
        kernel,
        out_shape=jax.ShapeDtypeStruct(eigenvectors.shape, F32),
        in_specs=[anywhere, anywhere, near],
        out_specs=anywhere,
        scratch_shapes=scratch,
        compiler_params=pltpu.CompilerParams(
            collective_id=0, has_side_effects=True, vmem_limit_bytes=60 * 1024 * 1024),
        cost_estimate=pl.CostEstimate(flops=flops, bytes_accessed=16 * 1024 * 1024, transcendentals=0),
    )(eigenvectors, packed, whole)


def product(spec, left_side, right_side):
    return jnp.einsum(spec, left_side, right_side, precision=lax.Precision.HIGH)


def adjoint_transposed(columns, vectors):
    spec = "nm,...nk->...mk"
    real_part = product(spec, columns[0], vectors[..., 0, :, :]) + product(spec, columns[1], vectors[..., 1, :, :])
    imag_part = product(spec, columns[1], vectors[..., 0, :, :]) - product(spec, columns[0], vectors[..., 1, :, :])
    return jnp.stack([real_part, imag_part], axis=-3)


def complex_rows(spec, left_side, right_side):
    real_part = product(spec, left_side[0], right_side[0]) - product(spec, left_side[1], right_side[1])
    imag_part = product(spec, left_side[0], right_side[1]) + product(spec, left_side[1], right_side[0])
    return jnp.stack([real_part, imag_part])


def merged_shards(eigenvectors, reflectors, reflector_factors):
    block_count, _, rows, share = reflectors.shape
    vectors = lax.all_gather(reflectors, "col", axis=3, tiled=True)
    width = vectors.shape[3]
    grams = []
    for block in range(block_count - 1):
        later = jnp.concatenate([reflectors[c] for c in range(block + 1, block_count)], axis=2)
        grams.append(adjoint_transposed(later, vectors[block]))
    gram = lax.psum(jnp.concatenate(grams, axis=1), "row")
    gram = gram.reshape(2, -1, share, width)
    gram = lax.all_gather(gram, "col", axis=2, tiled=True)
    projected = lax.psum_scatter(
        adjoint_transposed(eigenvectors, vectors), "row", scatter_dimension=2, tiled=True
    )
    results = [None] * block_count
    for block in reversed(range(block_count)):
        start = sum(block_count - 1 - b for b in range(block))
        sums = projected[block]
        for c in range(block + 1, block_count):
            sums = sums - complex_rows("mk,kj->mj", results[c], gram[:, start + c - block - 1])
        results[block] = complex_rows("mk,jk->mj", sums, reflector_factors[block])
    result = lax.all_gather(jnp.concatenate(results, axis=2), "row", axis=1, tiled=True)
    flat = vectors.transpose(1, 2, 0, 3).reshape(2, rows, block_count * width)
    return eigenvectors - complex_rows("nk,mk->nm", flat, result)


def solution(mesh):
    placed = (P(None, "row", "col"), P(None, None, "row", "col"), P())
    fused = mesh.shape["row"] == 2 ** BITS and mesh.shape["col"] == 2
    return jax.shard_map(
        fused_shards if fused else merged_shards, mesh=mesh, in_specs=placed, out_specs=P(None, "row", "col"), check_vma=False
    )
```

```python
import jax
import jax.numpy as jnp
from jax import lax
from jax.experimental import pallas as pl
from jax.experimental.pallas import tpu as pltpu
from jax.sharding import PartitionSpec as P

F32 = jnp.float32
BF16 = jnp.bfloat16
BITS = 4
GRAM = 4
ORDERS = {3: (0, 1, 2, 3), 2: (1, 2, 0, 3), GRAM: (1, 0, 2, 3), 1: (2, 0, 1, 3), 0: (0, 1, 2, 3)}


def split(value):
    high = value.astype(BF16)
    return high, (value - high.astype(F32)).astype(BF16)


def dot(left, right):
    return jnp.dot(left, right, preferred_element_type=F32)


def dot_lanes(left, right):
    return lax.dot_general(left, right, (((1,), (1,)), ((), ())), preferred_element_type=F32)


def kernel(z_hbm, v_hbm, factors, out_hbm, z, zt, w_own, w_other, vt, forms, acc, gacc,
           slots, gslots, xt, gx, gother, xk, gram, fact, z_sem, v_sem, out_sem, pair_send, pair_recv,
           row_send, row_recv):
    rows, columns = z.shape[1], z.shape[2]
    blocks = w_own.shape[0]
    share = w_own.shape[1] // 2
    row, col = lax.axis_index("row"), lax.axis_index("col")
    mine = [lax.rem(row // (1 << bit), 2) for bit in range(BITS)]
    partner = [row + (1 << bit) * (1 - 2 * mine[bit]) for bit in range(BITS)]
    sibling = {"row": row, "col": 1 - col}

    z_in = [pltpu.make_async_copy(z_hbm.at[p], z.at[p], z_sem.at[p]) for p in range(2)]
    v_in = [pltpu.make_async_copy(v_hbm.at[b], w_own.at[b], v_sem.at[b]) for b in range(blocks)]
    for b in reversed(range(blocks)):
        v_in[b].start()
    for copy in z_in:
        copy.start()

    barrier = pltpu.get_barrier_semaphore()
    for bit in range(BITS):
        pl.semaphore_signal(barrier, inc=1, device_id={"row": partner[bit], "col": col},
                            device_id_type=pl.DeviceIdType.MESH)
    pl.semaphore_signal(barrier, inc=1, device_id=sibling, device_id_type=pl.DeviceIdType.MESH)
    pl.semaphore_wait(barrier, BITS + 1)

    sends = []

    def send(source, target, send_sem, recv_sem, device):
        copy = pltpu.make_async_remote_copy(
            src_ref=source, dst_ref=target, send_sem=send_sem, recv_sem=recv_sem,
            device_id=device, device_id_type=pl.DeviceIdType.MESH)
        copy.start()
        sends.append(copy)
        return copy

    v_copies = {}
    for b in reversed(range(blocks)):
        v_in[b].wait()
        v_copies[b] = send(w_own.at[b], w_other.at[b], pair_send.at[b], pair_recv.at[b], sibling)

    @pl.loop(0, rows // 128)
    def _(step):
        part = pl.ds(pl.multiple_of(step * 128, 128), 128)
        for b in range(blocks):
            high, low = split(w_own[b, :, part])
            for p in range(2):
                vt[0, p, b * share:(b + 1) * share, part] = high[p * share:(p + 1) * share]
                vt[1, p, b * share:(b + 1) * share, part] = low[p * share:(p + 1) * share]

    for copy in z_in:
        copy.wait()

    @pl.loop(0, rows // 128)
    def _(step):
        part = pl.ds(pl.multiple_of(step * 128, 128), 128)
        for p in range(2):
            high, low = split(z[p, part, :].T)
            zt[0, p, :, part] = high
            zt[1, p, :, part] = low

    lane = lax.broadcasted_iota(jnp.int32, (1, 128), 1)
    sign = jnp.where(lane < share, 1.0, -1.0).astype(F32)

    for b in range(blocks):
        real, imag = factors[b, 0], factors[b, 1]
        real_turned, imag_turned = pltpu.roll(real, share, 1), pltpu.roll(imag, share, 1)
        first = lane < share
        parts = (
            (jnp.where(first, real, -imag_turned), jnp.where(first, real_turned, -imag)),
            (jnp.where(first, imag, real_turned), jnp.where(first, imag_turned, real)),
        )
        for h in range(2):
            for p in range(2):
                base = h * 2 * share + p * share
                for k in range(2):
                    fact[b, base:base + share, k * 128:(k + 1) * 128] = parts[p][k][h * share:(h + 1) * share]

    def make_forms(b):
        v_copies[b].wait_recv()

        @pl.loop(0, rows // 256)
        def _(step):
            part = pl.ds(pl.multiple_of(step * 256, 256), 256)
            own, other = w_own[b, :, part], w_other[b, :, part]
            halves = (jnp.where(col == 0, own, other).T, jnp.where(col == 0, other, own).T)
            for h in range(2):
                lanes = slice(b * 256 + h * 128, b * 256 + h * 128 + 128)
                for form, value in ((0, halves[h] * sign), (1, pltpu.roll(halves[h], share, 1))):
                    high, low = split(value)
                    forms[form, 0, part, lanes] = high
                    forms[form, 1, part, lanes] = low

    def products(turned, b, first, count):
        def body(step, total):
            part = pl.ds(pl.multiple_of(step * 256, 256), 256)
            for p in range(2):
                high = turned[0, p, first:first + count, part]
                low = turned[1, p, first:first + count, part]
                f_high = forms[p, 0, part, b * 256:(b + 1) * 256]
                f_low = forms[p, 1, part, b * 256:(b + 1) * 256]
                total = total + dot(high, f_high) + dot(high, f_low) + dot(low, f_high)
            return total

        return lax.fori_loop(0, rows // 256, body, jnp.zeros((count, 256), F32))

    def place(ref, prefix, free, fixed):
        at = list(prefix)
        for bit in reversed(range(BITS)):
            at.append(slice(None) if bit in free else fixed[bit])
        return ref.at[tuple(at)]

    def buffers(chunk):
        if chunk == GRAM:
            return gacc, (), gslots, (), gx
        return acc, (chunk,), slots, (chunk,), xt

    pending = {}

    def start_reduce(chunk, step):
        source, prefix, slot, slot_prefix, _ = buffers(chunk)
        order = ORDERS[chunk]
        fixed = dict(enumerate(mine))
        fixed[order[step]] = 1 - mine[order[step]]
        target = slot[step].at[slot_prefix] if slot_prefix else slot[step]
        pending[chunk] = send(
            place(source, prefix, order[step + 1:], fixed), target,
            row_send.at[chunk, step], row_recv.at[chunk, step],
            {"row": partner[order[step]], "col": col})

    def finish_reduce(chunk, step):
        source, prefix, slot, slot_prefix, _ = buffers(chunk)
        order = ORDERS[chunk]
        pending[chunk].wait_recv()
        held = place(source, prefix, order[step + 1:], dict(enumerate(mine)))
        arrived = slot[step].at[slot_prefix] if slot_prefix else slot[step]
        held[...] = held[...] + arrived[...]

    def start_spread(chunk, step):
        _, prefix, _, _, target = buffers(chunk)
        order = ORDERS[chunk][::-1]
        part = place(target, prefix, order[:step], dict(enumerate(mine)))
        pending[chunk] = send(
            part, part, row_send.at[chunk, BITS + step], row_recv.at[chunk, BITS + step],
            {"row": partner[order[step]], "col": col})

    def own_part(ref, prefix):
        return place(ref, prefix, (), dict(enumerate(mine)))

    def finish_gram():
        gram_copy.wait_recv()
        start = 0
        for b in range(blocks - 1):
            for c in range(b + 1, blocks):
                for group in range(share // 8):
                    q = (start * share) // 8 + group
                    owner, sub = q // 3, q % 3
                    at = (owner // 8, (owner // 4) % 2, (owner // 2) % 2, owner % 2, sub)
                    own, other = gx[at], gother[at]
                    halves = (jnp.where(col == 0, own, other), jnp.where(col == 0, other, own))
                    for h in range(2):
                        base = h * 2 * share + group * 8
                        gram[start, base:base + 8, :] = halves[h]
                        turned = jnp.concatenate(
                            [pltpu.roll(halves[h][:, k:k + 128], share, 1) * -sign for k in (0, 128)], axis=1)
                        gram[start, base + share:base + share + 8, :] = turned
                start += 1

    def dot3(left, high, low):
        l_high, l_low = split(left)
        return dot(l_high, high) + dot(l_high, low) + dot(l_low, high)

    solved = {}

    def solve(b):
        sums = own_part(acc, (b,))[...]
        start = sum(blocks - 1 - k for k in range(b))
        for c in range(b + 1, blocks):
            high, low = split(gram[start + c - b - 1])
            sums = sums - dot3(solved[c], high, low)
        s_high, s_low = split(sums)
        high, low = split(fact[b])
        solved[b] = dot_lanes(s_high, high) + dot_lanes(s_high, low) + dot_lanes(s_low, high)
        own_part(xt, (b,))[...] = solved[b]

    stage = {}

    def advance(chunk):
        nonlocal gram_copy
        step = stage[chunk]
        if step < BITS:
            finish_reduce(chunk, step)
            if step + 1 < BITS:
                start_reduce(chunk, step + 1)
            elif chunk == GRAM:
                own_part(gx, ())[...] = own_part(gacc, ())[...]
                start_spread(chunk, 0)
            elif chunk == blocks - 1:
                solve(chunk)
                start_spread(chunk, 0)
        elif step < 2 * BITS:
            pending[chunk].wait_recv()
            if step + 1 < 2 * BITS:
                start_spread(chunk, step + 1 - BITS)
            elif chunk == GRAM:
                gram_copy = send(gx, gother, pair_send.at[GRAM], pair_recv.at[GRAM], sibling)
        stage[chunk] += 1

    gram_copy = None

    def begin(chunk):
        if chunk == GRAM:
            q = 0
            for b in range(blocks - 1):
                count = share * (blocks - 1 - b)
                value = products(vt, b, share * (b + 1), count)
                for group in range(count // 8):
                    owner, sub = q // 3, q % 3
                    gacc[owner // 8, (owner // 4) % 2, (owner // 2) % 2, owner % 2, sub] = (
                        value[group * 8:group * 8 + 8])
                    q += 1
        else:
            value = products(zt, chunk, 0, columns)
            acc[chunk] = value.reshape(acc.shape[1:])
        start_reduce(chunk, 0)
        stage[chunk] = 0

    make_forms(3)
    begin(3)
    make_forms(2)
    begin(2)
    make_forms(1)
    make_forms(0)
    begin(GRAM)
    begin(1)
    advance(3)
    begin(0)
    for chunk in (2, GRAM, 3, 1, 0):
        advance(chunk)
    while stage[GRAM] < 2 * BITS:
        for chunk in (3, 2, GRAM, 1, 0):
            limit = 2 * BITS if chunk in (3, GRAM) else BITS
            if stage[chunk] < limit:
                advance(chunk)
    finish_gram()
    for b in (2, 1, 0):
        solve(b)
        start_spread(b, 0)

    def take(b):
        high, low = split(xt[b].reshape(columns, 256))
        xk[0, :, b * 256:(b + 1) * 256] = high
        xk[1, :, b * 256:(b + 1) * 256] = low

    def update(first, count, last):
        lanes = slice(first * 256, (first + count) * 256)

        @pl.loop(0, rows // 256)
        def _(step):
            part = pl.ds(pl.multiple_of(step * 256, 256), 256)
            for p in range(2):
                f_high, f_low = forms[p, 0, part, lanes], forms[p, 1, part, lanes]
                x_high, x_low = xk[0, :, lanes], xk[1, :, lanes]
                z[p, part, :] = z[p, part, :] - (
                    dot_lanes(f_high, x_high) + dot_lanes(f_high, x_low) + dot_lanes(f_low, x_high))
                if last:
                    pltpu.make_async_copy(
                        z.at[p, part, :], out_hbm.at[p, part, :], out_sem.at[p, step]).start()

    for _ in range(BITS - 1):
        for b in (2, 1, 0):
            advance(b)
    advance(2)
    take(3)
    take(2)
    update(2, 2, False)
    advance(1)
    advance(0)
    take(1)
    take(0)
    update(0, 2, True)
    for copy in sends:
        copy.wait_send()

    @pl.loop(0, rows // 256)
    def _(step):
        part = pl.ds(pl.multiple_of(step * 256, 256), 256)
        for p in range(2):
            pltpu.make_async_copy(z.at[p, part, :], out_hbm.at[p, part, :], out_sem.at[p, step]).wait()


def fused_shards(eigenvectors, reflectors, reflector_factors):
    blocks, _, rows, share = reflectors.shape
    columns = eigenvectors.shape[2]
    width = reflector_factors.shape[2]
    packed = jnp.swapaxes(reflectors, 2, 3).reshape(blocks, 2 * share, rows)
    two = (2,) * BITS
    owned = columns // 2 ** BITS
    vmem = pltpu.VMEM
    dma = pltpu.SemaphoreType.DMA
    slot_shapes = [vmem((blocks,) + (2,) * (BITS - 1 - s) + (owned, 2 * width), F32) for s in range(BITS)]
    gslot_shapes = [vmem((2,) * (BITS - 1 - s) + (3, 8, 2 * width), F32) for s in range(BITS)]
    scratch = [
        vmem((2, rows, columns), F32),
        vmem((2, 2, columns, rows), BF16),
        vmem((blocks, width, rows), F32),
        vmem((blocks, width, rows), F32),
        vmem((2, 2, blocks * share, rows), BF16),
        vmem((2, 2, rows, blocks * 2 * width), BF16),
        vmem((blocks,) + two + (owned, 2 * width), F32),
        vmem(two + (3, 8, 2 * width), F32),
        slot_shapes,
        gslot_shapes,
        vmem((blocks,) + two + (owned, 2 * width), F32),
        vmem(two + (3, 8, 2 * width), F32),
        vmem(two + (3, 8, 2 * width), F32),
        vmem((2, columns, blocks * 2 * width), BF16),
        vmem((6, 2 * width, 2 * width), F32),
        vmem((blocks, 2 * width, 2 * width), F32),
        dma((2,)),
        dma((blocks,)),
        dma((2, rows // 256)),
        dma((blocks + 1,)),
        dma((blocks + 1,)),
        dma((blocks + 1, 2 * BITS)),
        dma((blocks + 1, 2 * BITS)),
    ]
    anywhere = pl.BlockSpec(memory_space=pl.ANY)
    near = pl.BlockSpec(memory_space=pltpu.VMEM)
    flops = 2 * 2 * 3 * 4 * blocks * width * rows * columns
    return pl.pallas_call(
        kernel,
        out_shape=jax.ShapeDtypeStruct(eigenvectors.shape, F32),
        in_specs=[anywhere, anywhere, near],
        out_specs=anywhere,
        scratch_shapes=scratch,
        compiler_params=pltpu.CompilerParams(
            collective_id=0, has_side_effects=True, vmem_limit_bytes=60 * 1024 * 1024),
        cost_estimate=pl.CostEstimate(flops=flops, bytes_accessed=16 * 1024 * 1024, transcendentals=0),
    )(eigenvectors, packed, reflector_factors)


def product(spec, left_side, right_side):
    return jnp.einsum(spec, left_side, right_side, precision=lax.Precision.HIGH)


def adjoint_transposed(columns, vectors):
    spec = "nm,...nk->...mk"
    real_part = product(spec, columns[0], vectors[..., 0, :, :]) + product(spec, columns[1], vectors[..., 1, :, :])
    imag_part = product(spec, columns[1], vectors[..., 0, :, :]) - product(spec, columns[0], vectors[..., 1, :, :])
    return jnp.stack([real_part, imag_part], axis=-3)


def complex_rows(spec, left_side, right_side):
    real_part = product(spec, left_side[0], right_side[0]) - product(spec, left_side[1], right_side[1])
    imag_part = product(spec, left_side[0], right_side[1]) + product(spec, left_side[1], right_side[0])
    return jnp.stack([real_part, imag_part])


def merged_shards(eigenvectors, reflectors, reflector_factors):
    block_count, _, rows, share = reflectors.shape
    vectors = lax.all_gather(reflectors, "col", axis=3, tiled=True)
    width = vectors.shape[3]
    grams = []
    for block in range(block_count - 1):
        later = jnp.concatenate([reflectors[c] for c in range(block + 1, block_count)], axis=2)
        grams.append(adjoint_transposed(later, vectors[block]))
    gram = lax.psum(jnp.concatenate(grams, axis=1), "row")
    gram = gram.reshape(2, -1, share, width)
    gram = lax.all_gather(gram, "col", axis=2, tiled=True)
    projected = lax.psum_scatter(
        adjoint_transposed(eigenvectors, vectors), "row", scatter_dimension=2, tiled=True
    )
    results = [None] * block_count
    for block in reversed(range(block_count)):
        start = sum(block_count - 1 - b for b in range(block))
        sums = projected[block]
        for c in range(block + 1, block_count):
            sums = sums - complex_rows("mk,kj->mj", results[c], gram[:, start + c - block - 1])
        results[block] = complex_rows("mk,jk->mj", sums, reflector_factors[block])
    result = lax.all_gather(jnp.concatenate(results, axis=2), "row", axis=1, tiled=True)
    flat = vectors.transpose(1, 2, 0, 3).reshape(2, rows, block_count * width)
    return eigenvectors - complex_rows("nk,mk->nm", flat, result)


def solution(mesh):
    placed = (P(None, "row", "col"), P(None, None, "row", "col"), P())
    fused = mesh.shape["row"] == 2 ** BITS and mesh.shape["col"] == 2
    return jax.shard_map(
        fused_shards if fused else merged_shards, mesh=mesh, in_specs=placed, out_specs=P(None, "row", "col"), check_vma=False
    )
```
